512 devices in a mesh: row: 16 (over z_hi, x), col: 8 (over z_lo, core), layer: 4 (over y).
Axes of the slice: x: 4, y: 4, z: 16 (z_hi: 4, z_lo: 4; z = z_hi * 4 + z_lo), core: 2. Of those that a mesh axis runs over, the one named last changes fastest.
Arguments:
- blocks: bfloat16 [2048, 128, 128], P(('row', 'col')), may hold values from -2 to 2
- left_pick: int32 [2048], P(('row', 'col', 'layer')), may hold values from 0 to 15, as said below
- right_pick: int32 [2048], P(('row', 'col', 'layer')), may hold values from 0 to 15, as said below
- term_left: int32 [8192, 24], P(('row', 'col', 'layer')), may hold values from 0 to 31
- term_right: int32 [8192, 24], P(('row', 'col', 'layer')), may hold values from 0 to 63
- term_count: int32 [8192], P(('row', 'col', 'layer')), may hold values from 1 to 24
Outputs:
- product: float32 [2048, 128, 128], P(('row', 'col', 'layer'))
The draws below stay inside these ranges and needn't reach their ends.
Inputs may be any that keep to these rules, and one draw needn't show every extreme that they name: `left_pick`: for each tile, the 4 lists of 4 slots together name each of the tile's 16 slots exactly once. `right_pick`: for each tile, the 4 lists of 4 slots together name each of the tile's 16 slots exactly once.
All inputs are finite; a program needn't handle non-finite values.
Results may differ from the reference program's by a relative error of at most 0.0003.
Values may be sent and summed in bfloat16 or wider, within the bound.
A program may use at most 64 MiB of HBM per device.

```python
import jax
import jax.numpy as jnp
from jax import lax

BS = 128
SLOTS = 16
TERMS = 24
PICK = 4
TILES = 128
N_ROW = 16
N_COL = 8
N_LAYER = 4


def split_slots(key):
    keys = jax.random.split(key, N_ROW * N_COL)
    orders = jax.vmap(lambda k: jax.random.permutation(k, SLOTS))(keys)
    return orders.reshape(N_ROW * N_COL * N_LAYER * PICK).astype(jnp.int32)


def draw_left_pick(key, part):
    key = jax.random.fold_in(key, 11)
    return split_slots(key)


def draw_right_pick(key, part):
    key = jax.random.fold_in(key, 23)
    return split_slots(key)


def draw_term_count(key, part):
    key = jax.random.fold_in(key, 37)
    key_top, key_each, key_spot = jax.random.split(key, 3)
    devices_all = N_ROW * N_COL * N_LAYER
    highest = jax.random.randint(key_top, (devices_all, 1), max(1, TERMS // 4), TERMS + 1)
    counts = jax.random.randint(key_each, (devices_all, SLOTS), 1, highest + 1)
    counts = counts.reshape(devices_all * SLOTS)
    spot = jax.random.randint(key_spot, (), 0, devices_all * SLOTS)
    counts = counts.at[spot].set(TERMS)
    return counts.astype(jnp.int32)


def with_ends(values, stream_key, least, largest):
    longest = values.shape.index(max(values.shape))
    spots = []
    for shift in (0, 1):
        where = [jax.random.randint(jax.random.fold_in(stream_key, axis), (), 0, length) for axis, length in enumerate(values.shape)]
        where[longest] = (where[longest] + shift) % values.shape[longest]
        spots.append(tuple(where))
    return values.at[spots[0]].set(least).at[spots[1]].set(largest)


def steps_of(key, dims, cuts, smallest, largest):
    level, own = 1.0, jax.random.fold_in(key, 6)
    for position, shards_of in cuts:
        draws = jnp.exp(jax.random.uniform(jax.random.fold_in(own, position), (shards_of,), jnp.float32, smallest / len(cuts), largest / len(cuts)))
        level = level * jnp.repeat(draws, dims[position] // shards_of).reshape([-1 if axis == position else 1 for axis in range(len(dims))])
    return level


def gaussian(rng, extent, spread, most, cuts=(), kind=jnp.bfloat16):
    array = jax.random.normal(rng, extent, jnp.float32) * spread
    if len(cuts) > 0:
        array = steps_of(rng, extent, cuts, -0.22, 0.18) * array
    return jnp.clip(array, min=-most, max=most).astype(kind)


def setup_inputs(seed: int = 0) -> dict:
    streams_of = jax.random.split(jax.random.key(seed), 7)
    return {
        "blocks": gaussian(streams_of[0], (TILES * SLOTS, BS, BS), ((BS * TERMS) ** -0.25), 2.0, ((0, 128),)),
        "left_pick": draw_left_pick(jax.random.fold_in(streams_of[6], 71), 0),
        "right_pick": draw_right_pick(jax.random.fold_in(streams_of[6], 71), 0),
        "term_left": with_ends(jax.random.randint(streams_of[3], (TILES * N_LAYER * SLOTS, TERMS), 0, N_COL * PICK), jax.random.fold_in(streams_of[3], 1), 0, (N_COL * PICK) - 1).astype(jnp.int32),
        "term_right": with_ends(jax.random.randint(streams_of[4], (TILES * N_LAYER * SLOTS, TERMS), 0, N_ROW * PICK), jax.random.fold_in(streams_of[4], 1), 0, (N_ROW * PICK) - 1).astype(jnp.int32),
        "term_count": draw_term_count(jax.random.fold_in(streams_of[6], 71), 0),
    }


def reference(blocks, left_pick, right_pick, term_left, term_right, term_count):
    tiles = blocks.reshape(N_ROW, N_COL, SLOTS, BS, BS)
    left_lists = left_pick.reshape(N_ROW, N_COL, N_LAYER, PICK)
    right_lists = right_pick.reshape(N_ROW, N_COL, N_LAYER, PICK)
    left_terms = term_left.reshape(N_ROW, N_COL, N_LAYER, SLOTS, TERMS)
    right_terms = term_right.reshape(N_ROW, N_COL, N_LAYER, SLOTS, TERMS)
    counts = term_count.reshape(N_ROW, N_COL, N_LAYER, SLOTS)
    col_ids = jnp.arange(N_COL).astype(jnp.int32)[:, None]
    row_ids = jnp.arange(N_ROW).astype(jnp.int32)[:, None]
    term_ids = jnp.arange(TERMS).astype(jnp.int32)[None, :]

    def one_tile(index):
        row_now = index // N_COL
        col_now = index % N_COL
        row_tiles = tiles[row_now]
        col_tiles = tiles[:, col_now]

        def one_layer(total, layer):
            left_panel = row_tiles[col_ids, left_lists[row_now, :, layer]].reshape(N_COL * PICK, BS, BS)
            right_panel = col_tiles[row_ids, right_lists[:, col_now, layer]].reshape(N_ROW * PICK, BS, BS)
            live = term_ids < counts[row_now, col_now, layer][:, None]
            left_sel = left_panel[left_terms[row_now, col_now, layer]].astype(jnp.float32)
            left_sel = jnp.where(live[:, :, None, None], left_sel, jnp.float32(0.0))
            right_sel = right_panel[right_terms[row_now, col_now, layer]].astype(jnp.float32)
            part = jnp.einsum('stik,stkj->sij', left_sel, right_sel, precision=lax.Precision.HIGHEST)
            return total + part, None

        total, _ = lax.scan(one_layer, jnp.zeros((SLOTS, BS, BS), jnp.float32), jnp.arange(N_LAYER).astype(jnp.int32))
        return total

    result = lax.map(one_tile, jnp.arange(N_ROW * N_COL).astype(jnp.int32))
    return result.reshape(N_ROW * N_COL * SLOTS, BS, BS)
```

```python
import functools

import jax
import jax.numpy as jnp
from jax import lax
from jax.experimental import pallas as pl
from jax.experimental.pallas import tpu as pltpu
from jax.sharding import PartitionSpec as P

MESH = pl.DeviceIdType.MESH
BS = 128
PICK = 4
SLOTS = 16
TERMS = 24
N_ROW = 16
N_COL = 8
N_LAYER = 4
N_LEFT = N_COL * PICK
N_RIGHT = N_ROW * PICK


def kernel(
    blocks,
    left_pick,
    right_pick,
    term_left,
    term_right,
    term_count,
    out,
    left,
    right,
    part,
    from_down,
    from_up,
    last_down,
    last_up,
    z_send,
    z_recv,
    x_send,
    x_recv,
    l_send,
    l_recv,
    c_send,
    c_recv,
    y_send,
    y_recv,
):
    row = lax.axis_index("row")
    col = lax.axis_index("col")
    layer = lax.axis_index("layer")
    z_hi, x = row // 4, row % 4
    z_lo, core = col // 2, col % 2

    def at_z(step):
        return (((z_hi + step) % 4) * 4 + x, col, layer)

    def at_x(step):
        return (z_hi * 4 + (x + step) % 4, col, layer)

    def at_line(step):
        return (row, ((z_lo + step) % 4) * 2 + core, layer)

    def at_y(step):
        return (row, col, (layer + step) % 4)

    sibling = (row, z_lo * 2 + 1 - core, layer)

    barrier = pltpu.get_barrier_semaphore()
    partners = [at_z(1), at_z(3), at_x(1), at_x(3), at_line(1), at_line(2), at_line(3), sibling, at_y(1), at_y(3)]
    for partner in partners:
        pl.semaphore_signal(barrier, inc=1, device_id=partner, device_id_type=MESH)
    for j in range(PICK):
        right[row * PICK + j] = blocks[right_pick[j]]
    for j in range(PICK):
        left[col * PICK + j] = blocks[left_pick[j]]
    left[N_LEFT] = jnp.zeros((BS, BS), jnp.bfloat16)
    pl.semaphore_wait(barrier, len(partners))

    def copy(ref, first, count, send, recv, target):
        return pltpu.make_async_remote_copy(
            src_ref=ref.at[pl.ds(first, count)],
            dst_ref=ref.at[pl.ds(first, count)],
            send_sem=send,
            recv_sem=recv,
            device_id=target,
            device_id_type=MESH,
        )

    def first_of(h, xx, half):
        return (((h + 4) % 4) * 4 + (xx + 4) % 4) * PICK + 2 * half

    def z_copy(h, half, step, k):
        return copy(right, first_of(h, x, half), 2, z_send.at[k], z_recv.at[k], at_z(step))

    def x_copy(dz, half, step, xx):
        k = (dz * 2 + half) * 2 + (0 if step == 1 else 1)
        return copy(right, first_of(z_hi + dz, xx, half), 2, x_send.at[k], x_recv.at[k], at_x(step))

    def x_forward(dz, half, step, xx):
        k = 16 + (dz * 2 + half) * 2 + (0 if step == 1 else 1)
        piece = 0 if step == 1 else 1
        return copy(right, first_of(z_hi + dz, xx, half) + piece, 1, x_send.at[k], x_recv.at[k], at_x(step))

    def x_start(dz, half):
        x_copy(dz, half, 1, x).start()
        x_copy(dz, half, 3, x).start()

    def x_pass(dz, half):
        x_copy(dz, half, 1, x - 1).wait_recv()
        x_forward(dz, half, 1, x - 1).start()
        x_copy(dz, half, 3, x + 1).wait_recv()
        x_forward(dz, half, 3, x + 1).start()

    def x_end(dz, half):
        x_forward(dz, half, 1, x - 2).wait_recv()
        x_forward(dz, half, 3, x + 2).wait_recv()

    def l_copy(step):
        return copy(left, col * PICK, PICK, l_send.at[step - 1], l_recv.at[step - 1], at_line(step))

    def l_arrive(step):
        first = (((z_lo + 4 - step) % 4) * 2 + core) * PICK
        copy(left, first, PICK, l_send.at[step - 1], l_recv.at[step - 1], at_line(step)).wait_recv()
        copy(left, first, PICK, c_send.at[step], c_recv.at[step], sibling).start()

    def c_arrive(step):
        first = (((z_lo + 4 - step) % 4) * 2 + 1 - core) * PICK
        return copy(left, first, PICK, c_send.at[step], c_recv.at[step], sibling)

    z_copy(z_hi, 0, 1, 0).start()
    z_copy(z_hi, 1, 3, 1).start()
    z_copy(z_hi, 1, 1, 2).start()
    z_copy(z_hi, 0, 3, 3).start()
    x_start(0, 0)
    x_start(0, 1)
    copy(left, col * PICK, PICK, c_send.at[0], c_recv.at[0], sibling).start()
    x_pass(0, 0)
    x_pass(0, 1)
    z_copy(z_hi + 3, 0, 1, 0).wait_recv()
    z_copy(z_hi + 3, 0, 1, 4).start()
    z_copy(z_hi + 1, 1, 3, 1).wait_recv()
    z_copy(z_hi + 1, 1, 3, 5).start()
    x_start(3, 0)
    x_start(1, 1)
    for step in (1, 3, 2):
        l_copy(step).start()
    x_pass(3, 0)
    x_pass(1, 1)
    z_copy(z_hi + 3, 1, 1, 2).wait_recv()
    x_start(3, 1)
    z_copy(z_hi + 1, 0, 3, 3).wait_recv()
    x_start(1, 0)
    x_pass(3, 1)
    x_pass(1, 0)
    z_copy(z_hi + 2, 0, 1, 4).wait_recv()
    x_start(2, 0)
    z_copy(z_hi + 2, 1, 3, 5).wait_recv()
    x_start(2, 1)
    x_pass(2, 0)
    x_pass(2, 1)
    for step in (1, 3, 2):
        l_arrive(step)
    for dz in (0, 3, 1, 2):
        for half in (0, 1):
            x_end(dz, half)
    for step in (0, 1, 3, 2):
        c_arrive(step).wait_recv()

    def product(s):
        count = term_count[s]
        total = None
        for t in range(0, TERMS, 2):
            ids = [jnp.where(t + i < count, term_left[s, t + i], N_LEFT) for i in range(2)]
            lhs = jnp.concatenate([left[i] for i in ids], axis=1)
            rhs = jnp.concatenate([right[term_right[s, t + i]] for i in range(2)], axis=0)
            now = jnp.dot(lhs, rhs, preferred_element_type=jnp.float32)
            total = now if total is None else total + now
        return total

    def y_copy(src, i, dst, j, k, step):
        return pltpu.make_async_remote_copy(
            src_ref=src.at[i],
            dst_ref=dst.at[j],
            send_sem=y_send.at[k],
            recv_sem=y_recv.at[k],
            device_id=at_y(step),
            device_id_type=MESH,
        )

    far = ((layer + 2) % 4) * PICK
    up = ((layer + 1) % 4) * PICK
    down = ((layer + 3) % 4) * PICK
    own = layer * PICK

    def far_up(j):
        return y_copy(part, far + j, from_down, j, j, 1)

    def far_down(j):
        return y_copy(part, far + 2 + j, from_up, j, 2 + j, 3)

    def near_up(j):
        return y_copy(part, up + j, last_down, j, 4 + j, 1)

    def near_down(j):
        return y_copy(part, down + j, last_up, j, 8 + j, 3)

    @pl.loop(0, 2)
    def _(j):
        part[far + j] = product(far + j)
        far_up(j).start()
        part[far + 2 + j] = product(far + 2 + j)
        far_down(j).start()

    @pl.loop(0, 2)
    def _(j):
        part[up + 2 + j] = product(up + 2 + j)
        near_up(2 + j).start()
        part[down + j] = product(down + j)
        near_down(j).start()

    @pl.loop(0, 2)
    def _(j):
        one = product(up + j)
        far_up(j).wait_recv()
        part[up + j] = one + from_down[j]
        near_up(j).start()
        two = product(down + 2 + j)
        far_down(j).wait_recv()
        part[down + 2 + j] = two + from_up[j]
        near_down(2 + j).start()

    @pl.loop(0, PICK)
    def _(j):
        part[own + j] = product(own + j)

    for j in (2, 3, 0, 1):
        near_up(j).wait_recv()
        near_down((j + 2) % 4).wait_recv()
    for j in range(PICK):
        out[j] = part[own + j] + last_down[j] + last_up[j]

    z_copy(z_hi, 0, 1, 0).wait_send()
    z_copy(z_hi, 1, 3, 1).wait_send()
    z_copy(z_hi, 1, 1, 2).wait_send()
    z_copy(z_hi, 0, 3, 3).wait_send()
    z_copy(z_hi + 3, 0, 1, 4).wait_send()
    z_copy(z_hi + 1, 1, 3, 5).wait_send()
    for dz in range(4):
        for half in range(2):
            for step in (1, 3):
                x_copy(dz, half, step, x).wait_send()
                x_forward(dz, half, step, x - 2 + step).wait_send()
    for step in (1, 2, 3):
        l_copy(step).wait_send()
    for step in range(4):
        c_arrive(step).wait_send()
    for j in range(2):
        far_up(j).wait_send()
        far_down(j).wait_send()
    for j in range(PICK):
        near_up(j).wait_send()
        near_down(j).wait_send()


def shards(blocks, left_pick, right_pick, term_left, term_right, term_count):
    smem = pl.BlockSpec(memory_space=pltpu.SMEM)
    vmem = pl.BlockSpec(memory_space=pltpu.VMEM)
    dma = pltpu.SemaphoreType.DMA
    return pl.pallas_call(
        kernel,
        out_shape=jax.ShapeDtypeStruct((PICK, BS, BS), jnp.float32),
        in_specs=[vmem] + [smem] * 5,
        out_specs=vmem,
        scratch_shapes=[
            pltpu.VMEM((N_LEFT + 1, BS, BS), jnp.bfloat16),
            pltpu.VMEM((N_RIGHT, BS, BS), jnp.bfloat16),
            pltpu.VMEM((SLOTS, BS, BS), jnp.float32),
            pltpu.VMEM((2, BS, BS), jnp.float32),
            pltpu.VMEM((2, BS, BS), jnp.float32),
            pltpu.VMEM((PICK, BS, BS), jnp.float32),
            pltpu.VMEM((PICK, BS, BS), jnp.float32),
            dma((6,)),
            dma((6,)),
            dma((32,)),
            dma((32,)),
            dma((3,)),
            dma((3,)),
            dma((4,)),
            dma((4,)),
            dma((12,)),
            dma((12,)),
        ],
        compiler_params=pltpu.CompilerParams(
            collective_id=0, has_side_effects=True, vmem_limit_bytes=32 * 1024 * 1024
        ),
    )(blocks, left_pick, right_pick, term_left, term_right, term_count)


def solution(mesh):
    every = ("row", "col", "layer")
    in_specs = (P(("row", "col"), None, None), P(every), P(every), P(every, None), P(every, None), P(every))
    out_specs = P(every, None, None)
    return jax.shard_map(shards, mesh=mesh, in_specs=in_specs, out_specs=out_specs, check_vma=False)
```

```python
import functools

import jax
import jax.numpy as jnp
from jax import lax
from jax.experimental import pallas as pl
from jax.experimental.pallas import tpu as pltpu
from jax.sharding import PartitionSpec as P

MESH = pl.DeviceIdType.MESH
BS = 128
PICK = 4
SLOTS = 16
TERMS = 24
N_ROW = 16
N_COL = 8
N_LAYER = 4
N_LEFT = N_COL * PICK
N_RIGHT = N_ROW * PICK


def kernel(
    blocks_in,
    left_pick_in,
    right_pick_in,
    term_left_in,
    term_right_in,
    term_count_in,
    out,
    blocks,
    left_pick,
    right_pick,
    term_left,
    term_right,
    term_count,
    in_sem,
    left,
    right,
    part,
    from_down,
    from_up,
    last_down,
    last_up,
    z_send,
    z_recv,
    x_send,
    x_recv,
    l_send,
    l_recv,
    c_send,
    c_recv,
    y_send,
    y_recv,
):
    row = lax.axis_index("row")
    col = lax.axis_index("col")
    layer = lax.axis_index("layer")
    z_hi, x = row // 4, row % 4
    z_lo, core = col // 2, col % 2

    def at_z(step):
        return (((z_hi + step) % 4) * 4 + x, col, layer)

    def at_x(step):
        return (z_hi * 4 + (x + step) % 4, col, layer)

    def at_line(step):
        return (row, ((z_lo + step) % 4) * 2 + core, layer)

    def at_y(step):
        return (row, col, (layer + step) % 4)

    sibling = (row, z_lo * 2 + 1 - core, layer)

    pairs = [
        (left_pick_in, left_pick),
        (right_pick_in, right_pick),
        (blocks_in, blocks),
        (term_left_in, term_left),
        (term_right_in, term_right),
        (term_count_in, term_count),
    ]
    loads = [pltpu.make_async_copy(src, dst, in_sem.at[i]) for i, (src, dst) in enumerate(pairs)]
    for load in loads:
        load.start()
    barrier = pltpu.get_barrier_semaphore()
    partners = [at_z(1), at_z(3), at_x(1), at_x(3), sibling, at_y(1), at_y(3)]
    for partner in partners:
        pl.semaphore_signal(barrier, inc=1, device_id=partner, device_id_type=MESH)

    @pl.when(z_lo < 3)
    def _():
        pl.semaphore_signal(barrier, inc=1, device_id=at_line(1), device_id_type=MESH)

    @pl.when(z_lo > 0)
    def _():
        pl.semaphore_signal(barrier, inc=1, device_id=at_line(3), device_id_type=MESH)

    for load in loads[:3]:
        load.wait()
    for j in range(PICK):
        right[row * PICK + j] = blocks[right_pick[j]]
    for j in range(PICK):
        left[col * PICK + j] = blocks[left_pick[j]]
    left[N_LEFT] = jnp.zeros((BS, BS), jnp.bfloat16)
    inner = jnp.where((z_lo > 0) & (z_lo < 3), 1, 0)
    pl.semaphore_wait(barrier, len(partners) + 1 + inner)

    def copy(ref, first, count, send, recv, target):
        return pltpu.make_async_remote_copy(
            src_ref=ref.at[pl.ds(first, count)],
            dst_ref=ref.at[pl.ds(first, count)],
            send_sem=send,
            recv_sem=recv,
            device_id=target,
            device_id_type=MESH,
        )

    def first_of(h, xx, half):
        return (((h + 4) % 4) * 4 + (xx + 4) % 4) * PICK + 2 * half

    def z_copy(h, half, step, k):
        return copy(right, first_of(h, x, half), 2, z_send.at[k], z_recv.at[k], at_z(step))

    def x_copy(dz, half, step, xx):
        k = (dz * 2 + half) * 2 + (0 if step == 1 else 1)
        return copy(right, first_of(z_hi + dz, xx, half), 2, x_send.at[k], x_recv.at[k], at_x(step))

    def x_forward(dz, half, step, xx):
        k = 16 + (dz * 2 + half) * 2 + (0 if step == 1 else 1)
        piece = 0 if step == 1 else 1
        return copy(right, first_of(z_hi + dz, xx, half) + piece, 1, x_send.at[k], x_recv.at[k], at_x(step))

    def x_start(dz, half):
        x_copy(dz, half, 1, x).start()
        x_copy(dz, half, 3, x).start()

    def x_pass(dz, half):
        x_copy(dz, half, 1, x - 1).wait_recv()
        x_forward(dz, half, 1, x - 1).start()
        x_copy(dz, half, 3, x + 1).wait_recv()
        x_forward(dz, half, 3, x + 1).start()

    def x_end(dz, half):
        x_forward(dz, half, 1, x - 2).wait_recv()
        x_forward(dz, half, 3, x + 2).wait_recv()

    def l_copy(place, step):
        k = 2 * place + (0 if step == 1 else 1)
        return copy(left, (place * 2 + core) * PICK, PICK, l_send.at[k], l_recv.at[place], at_line(step))

    def l_start():
        @pl.when(z_lo < 3)
        def _():
            l_copy(z_lo, 1).start()

        @pl.when(z_lo > 0)
        def _():
            l_copy(z_lo, 3).start()

    def c_copy(place, side):
        return copy(left, (place * 2 + side) * PICK, PICK, c_send.at[place], c_recv.at[place], sibling)

    def l_pass(distance):
        @pl.when(z_lo >= distance)
        def _():
            place = z_lo - distance
            l_copy(place, 1).wait_recv()

            @pl.when(z_lo < 3)
            def _():
                l_copy(place, 1).start()

            c_copy(place, core).start()

        @pl.when(z_lo + distance <= 3)
        def _():
            place = z_lo + distance
            l_copy(place, 3).wait_recv()

            @pl.when(z_lo > 0)
            def _():
                l_copy(place, 3).start()

            c_copy(place, core).start()

    z_copy(z_hi, 0, 1, 0).start()
    z_copy(z_hi, 1, 3, 1).start()
    x_start(0, 0)
    x_start(0, 1)
    c_copy(z_lo, core).start()
    x_pass(0, 0)
    x_pass(0, 1)
    z_copy(z_hi, 0, 1, 0).wait_send()
    z_copy(z_hi, 1, 1, 2).start()
    z_copy(z_hi, 1, 3, 1).wait_send()
    z_copy(z_hi, 0, 3, 3).start()
    l_start()
    z_copy(z_hi + 3, 0, 1, 0).wait_recv()
    x_start(3, 0)
    z_copy(z_hi + 1, 1, 3, 1).wait_recv()
    x_start(1, 1)
    x_pass(3, 0)
    x_pass(1, 1)
    z_copy(z_hi, 1, 1, 2).wait_send()
    z_copy(z_hi + 3, 0, 1, 4).start()
    z_copy(z_hi, 0, 3, 3).wait_send()
    z_copy(z_hi + 1, 1, 3, 5).start()
    z_copy(z_hi + 3, 1, 1, 2).wait_recv()
    x_start(3, 1)
    z_copy(z_hi + 1, 0, 3, 3).wait_recv()
    x_start(1, 0)
    l_pass(1)
    x_pass(3, 1)
    x_pass(1, 0)
    z_copy(z_hi + 2, 0, 1, 4).wait_recv()
    x_start(2, 0)
    z_copy(z_hi + 2, 1, 3, 5).wait_recv()
    x_start(2, 1)
    l_pass(2)
    x_pass(2, 0)
    x_pass(2, 1)
    l_pass(3)
    x_end(0, 0)
    x_end(0, 1)
    x_end(3, 0)
    x_end(1, 1)
    x_end(3, 1)
    x_end(1, 0)
    x_end(2, 0)
    x_end(2, 1)
    for place in range(4):
        c_copy(place, 1 - core).wait_recv()
    for load in loads[3:]:
        load.wait()

    def product(s):
        count = term_count[s]
        total = None
        for t in range(0, TERMS, 2):
            ids = [jnp.where(t + i < count, term_left[s, t + i], N_LEFT) for i in range(2)]
            lhs = jnp.concatenate([left[i] for i in ids], axis=1)
            rhs = jnp.concatenate([right[term_right[s, t + i]] for i in range(2)], axis=0)
            now = jnp.dot(lhs, rhs, preferred_element_type=jnp.float32)
            total = now if total is None else total + now
        return total

    def y_copy(src, i, dst, j, k, step):
        return pltpu.make_async_remote_copy(
            src_ref=src.at[i],
            dst_ref=dst.at[j],
            send_sem=y_send.at[k],
            recv_sem=y_recv.at[k],
            device_id=at_y(step),
            device_id_type=MESH,
        )

    far = ((layer + 2) % 4) * PICK
    up = ((layer + 1) % 4) * PICK
    down = ((layer + 3) % 4) * PICK
    own = layer * PICK

    def far_up(j):
        return y_copy(part, far + j, from_down, j, j, 1)

    def far_down(j):
        return y_copy(part, far + 2 + j, from_up, j, 2 + j, 3)

    def near_up(j):
        return y_copy(part, up + j, last_down, j, 4 + j, 1)

    def near_down(j):
        return y_copy(part, down + j, last_up, j, 8 + j, 3)

    @pl.loop(0, 2)
    def _(j):
        part[far + j] = product(far + j)
        far_up(j).start()
        part[far + 2 + j] = product(far + 2 + j)
        far_down(j).start()

    @pl.loop(0, 2)
    def _(j):
        part[up + 2 + j] = product(up + 2 + j)
        near_up(2 + j).start()
        part[down + j] = product(down + j)
        near_down(j).start()

    @pl.loop(0, 2)
    def _(j):
        one = product(up + j)
        far_up(j).wait_recv()
        part[up + j] = one + from_down[j]
        near_up(j).start()
        two = product(down + 2 + j)
        far_down(j).wait_recv()
        part[down + 2 + j] = two + from_up[j]
        near_down(2 + j).start()

    @pl.loop(0, PICK)
    def _(j):
        part[own + j] = product(own + j)

    for j in (2, 3, 0, 1):
        near_up(j).wait_recv()
        near_down((j + 2) % 4).wait_recv()
    for j in range(PICK):
        out[j] = part[own + j] + last_down[j] + last_up[j]

    z_copy(z_hi + 3, 0, 1, 4).wait_send()
    z_copy(z_hi + 1, 1, 3, 5).wait_send()
    for dz in range(4):
        for half in range(2):
            for step in (1, 3):
                x_copy(dz, half, step, x).wait_send()
                x_forward(dz, half, step, x - 2 + step).wait_send()
    for place in range(4):

        @pl.when((place <= z_lo) & (z_lo < 3))
        def _():
            l_copy(place, 1).wait_send()

        @pl.when((place >= z_lo) & (z_lo > 0))
        def _():
            l_copy(place, 3).wait_send()

        c_copy(place, core).wait_send()
    for j in range(2):
        far_up(j).wait_send()
        far_down(j).wait_send()
    for j in range(PICK):
        near_up(j).wait_send()
        near_down(j).wait_send()


def shards(*arrays):
    vmem = pl.BlockSpec(memory_space=pltpu.VMEM)
    dma = pltpu.SemaphoreType.DMA
    return pl.pallas_call(
        kernel,
        out_shape=jax.ShapeDtypeStruct((PICK, BS, BS), jnp.float32),
        in_specs=[pl.BlockSpec(memory_space=pl.ANY)] * 6,
        out_specs=vmem,
        scratch_shapes=[
            pltpu.VMEM((SLOTS, BS, BS), jnp.bfloat16),
            pltpu.SMEM((PICK,), jnp.int32),
            pltpu.SMEM((PICK,), jnp.int32),
            pltpu.SMEM((SLOTS, TERMS), jnp.int32),
            pltpu.SMEM((SLOTS, TERMS), jnp.int32),
            pltpu.SMEM((SLOTS,), jnp.int32),
            dma((6,)),
            pltpu.VMEM((N_LEFT + 1, BS, BS), jnp.bfloat16),
            pltpu.VMEM((N_RIGHT, BS, BS), jnp.bfloat16),
            pltpu.VMEM((SLOTS, BS, BS), jnp.float32),
            pltpu.VMEM((2, BS, BS), jnp.float32),
            pltpu.VMEM((2, BS, BS), jnp.float32),
            pltpu.VMEM((PICK, BS, BS), jnp.float32),
            pltpu.VMEM((PICK, BS, BS), jnp.float32),
            dma((6,)),
            dma((6,)),
            dma((32,)),
            dma((32,)),
            dma((8,)),
            dma((4,)),
            dma((4,)),
            dma((4,)),
            dma((12,)),
            dma((12,)),
        ],
        compiler_params=pltpu.CompilerParams(
            collective_id=0, has_side_effects=True, vmem_limit_bytes=32 * 1024 * 1024
        ),
    )(*[pltpu.with_memory_space_constraint(a, pltpu.HBM) for a in arrays])


def solution(mesh):
    every = ("row", "col", "layer")
    in_specs = (P(("row", "col"), None, None), P(every), P(every), P(every, None), P(every, None), P(every))
    out_specs = P(every, None, None)
    return jax.shard_map(shards, mesh=mesh, in_specs=in_specs, out_specs=out_specs, check_vma=False)
```

```python
import functools

import jax
import jax.numpy as jnp
from jax import lax
from jax.experimental import pallas as pl
from jax.experimental.pallas import tpu as pltpu
from jax.sharding import PartitionSpec as P

MESH = pl.DeviceIdType.MESH
BS = 128
PICK = 4
SLOTS = 16
TERMS = 24
LEVELS = 32760.0
EXTRA = 16
N_ROW = 16
N_COL = 8
N_LAYER = 4
N_LEFT = N_COL * PICK
N_RIGHT = N_ROW * PICK


def kernel(
    blocks_in,
    left_pick_in,
    right_pick_in,
    term_left_in,
    term_right_in,
    term_count_in,
    out,
    blocks,
    left_pick,
    right_pick,
    term_left,
    term_right,
    term_count,
    in_sem,
    left,
    right,
    part,
    packed,
    arrived,
    z_send,
    z_recv,
    x_send,
    x_recv,
    l_send,
    l_recv,
    c_send,
    c_recv,
    y_send,
    y_recv,
):
    row = lax.axis_index("row")
    col = lax.axis_index("col")
    layer = lax.axis_index("layer")
    z_hi, x = row // 4, row % 4
    z_lo, core = col // 2, col % 2

    def at_z(step):
        return (((z_hi + step) % 4) * 4 + x, col, layer)

    def at_x(step):
        return (z_hi * 4 + (x + step) % 4, col, layer)

    def at_line(step):
        return (row, ((z_lo + step) % 4) * 2 + core, layer)

    def at_y(step):
        return (row, col, (layer + step) % 4)

    sibling = (row, z_lo * 2 + 1 - core, layer)

    pairs = [
        (left_pick_in, left_pick),
        (right_pick_in, right_pick),
        (blocks_in, blocks),
        (term_left_in, term_left),
        (term_right_in, term_right),
        (term_count_in, term_count),
    ]
    loads = [pltpu.make_async_copy(src, dst, in_sem.at[i]) for i, (src, dst) in enumerate(pairs)]
    for load in loads:
        load.start()
    barrier = pltpu.get_barrier_semaphore()
    partners = [at_z(1), at_z(3), at_x(1), at_x(2), at_x(3), sibling, at_y(1), at_y(2), at_y(3)]
    for partner in partners:
        pl.semaphore_signal(barrier, inc=1, device_id=partner, device_id_type=MESH)

    @pl.when(z_lo < 3)
    def _():
        pl.semaphore_signal(barrier, inc=1, device_id=at_line(1), device_id_type=MESH)

    @pl.when(z_lo > 0)
    def _():
        pl.semaphore_signal(barrier, inc=1, device_id=at_line(3), device_id_type=MESH)

    for load in loads[:3]:
        load.wait()
    for j in range(PICK):
        right[row * PICK + j] = blocks[right_pick[j]]
    for j in range(PICK):
        left[col * PICK + j] = blocks[left_pick[j]]
    left[N_LEFT] = jnp.zeros((BS, BS), jnp.bfloat16)
    inner = jnp.where((z_lo > 0) & (z_lo < 3), 1, 0)
    pl.semaphore_wait(barrier, len(partners) + 1 + inner)

    def copy(ref, first, count, send, recv, target):
        return pltpu.make_async_remote_copy(
            src_ref=ref.at[pl.ds(first, count)],
            dst_ref=ref.at[pl.ds(first, count)],
            send_sem=send,
            recv_sem=recv,
            device_id=target,
            device_id_type=MESH,
        )

    def first_of(h, xx, half):
        return (((h + 4) % 4) * 4 + (xx + 4) % 4) * PICK + 2 * half

    def z_copy(h, half, step, k):
        return copy(right, first_of(h, x, half), 2, z_send.at[k], z_recv.at[k], at_z(step))

    def x_copy(dz, half, step, xx):
        k = (dz * 2 + half) * 3 + step - 1
        return copy(right, first_of(z_hi + dz, xx, half), 2, x_send.at[k], x_recv.at[k], at_x(step))

    def x_start(dz, half):
        for step in (1, 3, 2):
            x_copy(dz, half, step, x).start()

    def x_end(dz, half):
        for step in (1, 3, 2):
            x_copy(dz, half, step, x - step).wait_recv()

    def l_copy(place, step):
        k = 2 * place + (0 if step == 1 else 1)
        return copy(left, (place * 2 + core) * PICK, PICK, l_send.at[k], l_recv.at[place], at_line(step))

    def l_start():
        @pl.when(z_lo < 3)
        def _():
            l_copy(z_lo, 1).start()

        @pl.when(z_lo > 0)
        def _():
            l_copy(z_lo, 3).start()

    def c_copy(place, side):
        return copy(left, (place * 2 + side) * PICK, PICK, c_send.at[place], c_recv.at[place], sibling)

    def l_pass(distance):
        @pl.when(z_lo >= distance)
        def _():
            place = z_lo - distance
            l_copy(place, 1).wait_recv()

            @pl.when(z_lo < 3)
            def _():
                l_copy(place, 1).start()

            c_copy(place, core).start()

        @pl.when(z_lo + distance <= 3)
        def _():
            place = z_lo + distance
            l_copy(place, 3).wait_recv()

            @pl.when(z_lo > 0)
            def _():
                l_copy(place, 3).start()

            c_copy(place, core).start()

    z_copy(z_hi, 0, 1, 0).start()
    z_copy(z_hi, 1, 3, 1).start()
    x_start(0, 0)
    x_start(0, 1)
    c_copy(z_lo, core).start()
    z_copy(z_hi, 0, 1, 0).wait_send()
    z_copy(z_hi, 1, 1, 2).start()
    z_copy(z_hi, 1, 3, 1).wait_send()
    z_copy(z_hi, 0, 3, 3).start()
    l_start()
    z_copy(z_hi + 3, 0, 1, 0).wait_recv()
    x_start(3, 0)
    z_copy(z_hi + 1, 1, 3, 1).wait_recv()
    x_start(1, 1)
    z_copy(z_hi, 1, 1, 2).wait_send()
    z_copy(z_hi + 3, 0, 1, 4).start()
    z_copy(z_hi, 0, 3, 3).wait_send()
    z_copy(z_hi + 1, 1, 3, 5).start()
    z_copy(z_hi + 3, 1, 1, 2).wait_recv()
    x_start(3, 1)
    z_copy(z_hi + 1, 0, 3, 3).wait_recv()
    x_start(1, 0)
    l_pass(1)
    z_copy(z_hi + 2, 0, 1, 4).wait_recv()
    x_start(2, 0)
    l_pass(2)
    z_copy(z_hi + 2, 1, 3, 5).wait_recv()
    x_start(2, 1)
    l_pass(3)
    for dz in (0, 3, 1, 2):
        for half in range(2):
            x_end(dz, half)
    for place in range(4):
        c_copy(place, 1 - core).wait_recv()
    for load in loads[3:]:
        load.wait()

    def product(s):
        count = term_count[s]
        total = None
        for t in range(0, TERMS, 2):
            ids = [jnp.where(t + i < count, term_left[s, t + i], N_LEFT) for i in range(2)]
            lhs = jnp.concatenate([left[i] for i in ids], axis=1)
            rhs = jnp.concatenate([right[term_right[s, t + i]] for i in range(2)], axis=0)
            now = jnp.dot(lhs, rhs, preferred_element_type=jnp.float32)
            total = now if total is None else total + now
        return total

    def code(value):
        top = jnp.max(jnp.abs(value), axis=0, keepdims=True)
        power = jnp.clip(jnp.ceil(jnp.log2(top)), -120.0, 120.0)
        digits = jnp.floor(value * (jnp.exp2(-power) * LEVELS) + 0.5)
        return digits.astype(jnp.int32).astype(jnp.int16), jnp.broadcast_to(power, (EXTRA, BS)).astype(jnp.int32).astype(jnp.int16)

    def put(j, value):
        digits, power = code(value)
        packed[j, pl.ds(0, BS)] = digits
        packed[j, pl.ds(BS, EXTRA)] = power

    def get(ref, j):
        power = ref[j, pl.ds(BS, EXTRA)].astype(jnp.int32).astype(jnp.float32)[0:1]
        return ref[j, pl.ds(0, BS)].astype(jnp.int32).astype(jnp.float32) * (jnp.exp2(power) * (1.0 / LEVELS))

    def y_copy(i, dst, j, k, step):
        return pltpu.make_async_remote_copy(
            src_ref=packed.at[i],
            dst_ref=dst.at[j],
            send_sem=y_send.at[k],
            recv_sem=y_recv.at[k],
            device_id=at_y(step),
            device_id_type=MESH,
        )

    def sent(step, j):
        return y_copy((step - 1) * PICK + j, arrived, (step - 1) * PICK + j, (step - 1) * PICK + j, step)

    def send(step, picks):
        first = ((layer + step) % 4) * PICK
        for j, value in [(j, product(first + j)) for j in picks]:
            put((step - 1) * PICK + j, value)
        for j in picks:
            sent(step, j).start()

    send(2, (0, 1))
    send(2, (2, 3))
    send(1, (0, 1, 2, 3))
    send(3, (0, 1, 2, 3))
    for j in range(PICK):
        part[j] = product(layer * PICK + j)

    for j in range(PICK):
        total = part[j]
        for step in (2, 1, 3):
            sent(step, j).wait_recv()
            total += get(arrived, (step - 1) * PICK + j)
        out[j] = total

    z_copy(z_hi + 3, 0, 1, 4).wait_send()
    z_copy(z_hi + 1, 1, 3, 5).wait_send()
    for dz in range(4):
        for half in range(2):
            for step in (1, 2, 3):
                x_copy(dz, half, step, x).wait_send()
    for place in range(4):

        @pl.when((place <= z_lo) & (z_lo < 3))
        def _():
            l_copy(place, 1).wait_send()

        @pl.when((place >= z_lo) & (z_lo > 0))
        def _():
            l_copy(place, 3).wait_send()

        c_copy(place, core).wait_send()
    for step in (1, 2, 3):
        for j in range(PICK):
            sent(step, j).wait_send()


def shards(*arrays):
    vmem = pl.BlockSpec(memory_space=pltpu.VMEM)
    dma = pltpu.SemaphoreType.DMA
    return pl.pallas_call(
        kernel,
        out_shape=jax.ShapeDtypeStruct((PICK, BS, BS), jnp.float32),
        in_specs=[pl.BlockSpec(memory_space=pl.ANY)] * 6,
        out_specs=vmem,
        scratch_shapes=[
            pltpu.VMEM((SLOTS, BS, BS), jnp.bfloat16),
            pltpu.SMEM((PICK,), jnp.int32),
            pltpu.SMEM((PICK,), jnp.int32),
            pltpu.SMEM((SLOTS, TERMS), jnp.int32),
            pltpu.SMEM((SLOTS, TERMS), jnp.int32),
            pltpu.SMEM((SLOTS,), jnp.int32),
            dma((6,)),
            pltpu.VMEM((N_LEFT + 1, BS, BS), jnp.bfloat16),
            pltpu.VMEM((N_RIGHT, BS, BS), jnp.bfloat16),
            pltpu.VMEM((PICK, BS, BS), jnp.float32),
            pltpu.VMEM((3 * PICK, BS + EXTRA, BS), jnp.int16),
            pltpu.VMEM((3 * PICK, BS + EXTRA, BS), jnp.int16),
            dma((6,)),
            dma((6,)),
            dma((24,)),
            dma((24,)),
            dma((8,)),
            dma((4,)),
            dma((4,)),
            dma((4,)),
            dma((12,)),
            dma((12,)),
        ],
        compiler_params=pltpu.CompilerParams(
            collective_id=0, has_side_effects=True, vmem_limit_bytes=32 * 1024 * 1024
        ),
    )(*[pltpu.with_memory_space_constraint(a, pltpu.HBM) for a in arrays])


def solution(mesh):
    every = ("row", "col", "layer")
    in_specs = (P(("row", "col"), None, None), P(every), P(every), P(every, None), P(every, None), P(every))
    out_specs = P(every, None, None)
    return jax.shard_map(shards, mesh=mesh, in_specs=in_specs, out_specs=out_specs, check_vma=False)
```

```python
import functools

import jax
import jax.numpy as jnp
from jax import lax
from jax.experimental import pallas as pl
from jax.experimental.pallas import tpu as pltpu
from jax.sharding import PartitionSpec as P

MESH = pl.DeviceIdType.MESH
BS = 128
PICK = 4
SLOTS = 16
TERMS = 24
LEVELS = 32760.0
EXTRA = 16
N_ROW = 16
N_COL = 8
N_LAYER = 4
N_LEFT = N_COL * PICK
N_RIGHT = N_ROW * PICK


def kernel(
    blocks_in,
    left_pick_in,
    right_pick_in,
    term_left_in,
    term_right_in,
    term_count_in,
    out,
    blocks,
    left_pick,
    right_pick,
    term_left,
    term_right,
    term_count,
    in_sem,
    left,
    right,
    part,
    packed,
    from_down,
    from_up,
    last_down,
    last_up,
    z_send,
    z_recv,
    x_send,
    x_recv,
    l_send,
    l_recv,
    c_send,
    c_recv,
    y_send,
    y_recv,
):
    row = lax.axis_index("row")
    col = lax.axis_index("col")
    layer = lax.axis_index("layer")
    z_hi, x = row // 4, row % 4
    z_lo, core = col // 2, col % 2

    def at_z(step):
        return (((z_hi + step) % 4) * 4 + x, col, layer)

    def at_x(step):
        return (z_hi * 4 + (x + step) % 4, col, layer)

    def at_line(step):
        return (row, ((z_lo + step) % 4) * 2 + core, layer)

    def at_y(step):
        return (row, col, (layer + step) % 4)

    sibling = (row, z_lo * 2 + 1 - core, layer)

    pairs = [
        (left_pick_in, left_pick),
        (right_pick_in, right_pick),
        (blocks_in, blocks),
        (term_left_in, term_left),
        (term_right_in, term_right),
        (term_count_in, term_count),
    ]
    loads = [pltpu.make_async_copy(src, dst, in_sem.at[i]) for i, (src, dst) in enumerate(pairs)]
    for load in loads:
        load.start()
    barrier = pltpu.get_barrier_semaphore()
    partners = [at_z(1), at_z(3), at_x(1), at_x(2), at_x(3), sibling, at_y(1), at_y(3)]
    for partner in partners:
        pl.semaphore_signal(barrier, inc=1, device_id=partner, device_id_type=MESH)

    @pl.when(z_lo < 3)
    def _():
        pl.semaphore_signal(barrier, inc=1, device_id=at_line(1), device_id_type=MESH)

    @pl.when(z_lo > 0)
    def _():
        pl.semaphore_signal(barrier, inc=1, device_id=at_line(3), device_id_type=MESH)

    for load in loads[:3]:
        load.wait()
    for j in range(PICK):
        right[row * PICK + j] = blocks[right_pick[j]]
    for j in range(PICK):
        left[col * PICK + j] = blocks[left_pick[j]]
    left[N_LEFT] = jnp.zeros((BS, BS), jnp.bfloat16)
    inner = jnp.where((z_lo > 0) & (z_lo < 3), 1, 0)
    pl.semaphore_wait(barrier, len(partners) + 1 + inner)

    def copy(ref, first, count, send, recv, target):
        return pltpu.make_async_remote_copy(
            src_ref=ref.at[pl.ds(first, count)],
            dst_ref=ref.at[pl.ds(first, count)],
            send_sem=send,
            recv_sem=recv,
            device_id=target,
            device_id_type=MESH,
        )

    def first_of(h, xx, half):
        return (((h + 4) % 4) * 4 + (xx + 4) % 4) * PICK + 2 * half

    def z_copy(h, half, step, k):
        return copy(right, first_of(h, x, half), 2, z_send.at[k], z_recv.at[k], at_z(step))

    def x_copy(dz, half, step, xx):
        k = (dz * 2 + half) * 3 + step - 1
        return copy(right, first_of(z_hi + dz, xx, half), 2, x_send.at[k], x_recv.at[k], at_x(step))

    def x_start(dz, half):
        for step in (1, 3, 2):
            x_copy(dz, half, step, x).start()

    def x_end(dz, half):
        for step in (1, 3, 2):
            x_copy(dz, half, step, x - step).wait_recv()

    def l_copy(place, step):
        k = 2 * place + (0 if step == 1 else 1)
        return copy(left, (place * 2 + core) * PICK, PICK, l_send.at[k], l_recv.at[place], at_line(step))

    def l_start():
        @pl.when(z_lo < 3)
        def _():
            l_copy(z_lo, 1).start()

        @pl.when(z_lo > 0)
        def _():
            l_copy(z_lo, 3).start()

    def c_copy(place, side):
        return copy(left, (place * 2 + side) * PICK, PICK, c_send.at[place], c_recv.at[place], sibling)

    def l_pass(distance):
        @pl.when(z_lo >= distance)
        def _():
            place = z_lo - distance
            l_copy(place, 1).wait_recv()

            @pl.when(z_lo < 3)
            def _():
                l_copy(place, 1).start()

            c_copy(place, core).start()

        @pl.when(z_lo + distance <= 3)
        def _():
            place = z_lo + distance
            l_copy(place, 3).wait_recv()

            @pl.when(z_lo > 0)
            def _():
                l_copy(place, 3).start()

            c_copy(place, core).start()

    z_copy(z_hi, 0, 1, 0).start()
    z_copy(z_hi, 1, 3, 1).start()
    x_start(0, 0)
    x_start(0, 1)
    c_copy(z_lo, core).start()
    z_copy(z_hi, 0, 1, 0).wait_send()
    z_copy(z_hi, 1, 1, 2).start()
    z_copy(z_hi, 1, 3, 1).wait_send()
    z_copy(z_hi, 0, 3, 3).start()
    l_start()
    z_copy(z_hi + 3, 0, 1, 0).wait_recv()
    x_start(3, 0)
    z_copy(z_hi + 1, 1, 3, 1).wait_recv()
    x_start(1, 1)
    z_copy(z_hi, 1, 1, 2).wait_send()
    z_copy(z_hi + 3, 0, 1, 4).start()
    z_copy(z_hi, 0, 3, 3).wait_send()
    z_copy(z_hi + 1, 1, 3, 5).start()
    z_copy(z_hi + 3, 1, 1, 2).wait_recv()
    x_start(3, 1)
    z_copy(z_hi + 1, 0, 3, 3).wait_recv()
    x_start(1, 0)
    l_pass(1)
    z_copy(z_hi + 2, 0, 1, 4).wait_recv()
    x_start(2, 0)
    l_pass(2)
    z_copy(z_hi + 2, 1, 3, 5).wait_recv()
    x_start(2, 1)
    l_pass(3)
    for dz in (0, 3, 1, 2):
        for half in range(2):
            x_end(dz, half)
    for place in range(4):
        c_copy(place, 1 - core).wait_recv()
    for load in loads[3:]:
        load.wait()

    def product(s):
        count = term_count[s]
        total = None
        for t in range(0, TERMS, 2):
            ids = [jnp.where(t + i < count, term_left[s, t + i], N_LEFT) for i in range(2)]
            lhs = jnp.concatenate([left[i] for i in ids], axis=1)
            rhs = jnp.concatenate([right[term_right[s, t + i]] for i in range(2)], axis=0)
            now = jnp.dot(lhs, rhs, preferred_element_type=jnp.float32)
            total = now if total is None else total + now
        return total

    def code(value):
        top = jnp.max(jnp.abs(value), axis=0, keepdims=True)
        power = jnp.clip(jnp.ceil(jnp.log2(top)), -120.0, 120.0)
        digits = jnp.floor(value * (jnp.exp2(-power) * LEVELS) + 0.5)
        return digits.astype(jnp.int32).astype(jnp.int16), jnp.broadcast_to(power, (EXTRA, BS)).astype(jnp.int32).astype(jnp.int16)

    def put(j, value):
        digits, power = code(value)
        packed[j, pl.ds(0, BS)] = digits
        packed[j, pl.ds(BS, EXTRA)] = power

    def get(ref, j):
        power = ref[j, pl.ds(BS, EXTRA)].astype(jnp.int32).astype(jnp.float32)[0:1]
        return ref[j, pl.ds(0, BS)].astype(jnp.int32).astype(jnp.float32) * (jnp.exp2(power) * (1.0 / LEVELS))

    def y_copy(i, dst, j, k, step):
        return pltpu.make_async_remote_copy(
            src_ref=packed.at[i],
            dst_ref=dst.at[j],
            send_sem=y_send.at[k],
            recv_sem=y_recv.at[k],
            device_id=at_y(step),
            device_id_type=MESH,
        )

    far = ((layer + 2) % 4) * PICK
    up = ((layer + 1) % 4) * PICK
    down = ((layer + 3) % 4) * PICK
    own = layer * PICK

    def far_up(j):
        return y_copy(j, from_down, j, j, 1)

    def far_down(j):
        return y_copy(2 + j, from_up, j, 2 + j, 3)

    def near_up(j):
        return y_copy(4 + j, last_down, j, 4 + j, 1)

    def near_down(j):
        return y_copy(8 + j, last_up, j, 8 + j, 3)

    @pl.loop(0, 2)
    def _(j):
        one, two = product(far + j), product(far + 2 + j)
        put(j, one)
        put(2 + j, two)
        far_up(j).start()
        far_down(j).start()

    for j in range(2):
        put(6 + j, product(up + 2 + j))
        put(8 + j, product(down + j))
    for j in range(2):
        near_up(2 + j).start()
        near_down(j).start()
    sums = [(product(up + j), product(down + 2 + j)) for j in range(2)]
    for j in range(2):
        far_up(j).wait_recv()
        put(4 + j, sums[j][0] + get(from_down, j))
        near_up(j).start()
        far_down(j).wait_recv()
        put(10 + j, sums[j][1] + get(from_up, j))
        near_down(2 + j).start()
    for j in range(PICK):
        part[j] = product(own + j)
    for j in (2, 3, 0, 1):
        near_up(j).wait_recv()
        near_down((j + 2) % 4).wait_recv()
    for j in range(PICK):
        out[j] = part[j] + get(last_down, j) + get(last_up, j)

    z_copy(z_hi + 3, 0, 1, 4).wait_send()
    z_copy(z_hi + 1, 1, 3, 5).wait_send()
    for dz in range(4):
        for half in range(2):
            for step in (1, 2, 3):
                x_copy(dz, half, step, x).wait_send()
    for place in range(4):

        @pl.when((place <= z_lo) & (z_lo < 3))
        def _():
            l_copy(place, 1).wait_send()

        @pl.when((place >= z_lo) & (z_lo > 0))
        def _():
            l_copy(place, 3).wait_send()

        c_copy(place, core).wait_send()
    for j in range(2):
        far_up(j).wait_send()
        far_down(j).wait_send()
    for j in range(PICK):
        near_up(j).wait_send()
        near_down(j).wait_send()


def shards(*arrays):
    vmem = pl.BlockSpec(memory_space=pltpu.VMEM)
    dma = pltpu.SemaphoreType.DMA
    return pl.pallas_call(
        kernel,
        out_shape=jax.ShapeDtypeStruct((PICK, BS, BS), jnp.float32),
        in_specs=[pl.BlockSpec(memory_space=pl.ANY)] * 6,
        out_specs=vmem,
        scratch_shapes=[
            pltpu.VMEM((SLOTS, BS, BS), jnp.bfloat16),
            pltpu.SMEM((PICK,), jnp.int32),
            pltpu.SMEM((PICK,), jnp.int32),
            pltpu.SMEM((SLOTS, TERMS), jnp.int32),
            pltpu.SMEM((SLOTS, TERMS), jnp.int32),
            pltpu.SMEM((SLOTS,), jnp.int32),
            dma((6,)),
            pltpu.VMEM((N_LEFT + 1, BS, BS), jnp.bfloat16),
            pltpu.VMEM((N_RIGHT, BS, BS), jnp.bfloat16),
            pltpu.VMEM((PICK, BS, BS), jnp.float32),
            pltpu.VMEM((3 * PICK, BS + EXTRA, BS), jnp.int16),
            pltpu.VMEM((2, BS + EXTRA, BS), jnp.int16),
            pltpu.VMEM((2, BS + EXTRA, BS), jnp.int16),
            pltpu.VMEM((PICK, BS + EXTRA, BS), jnp.int16),
            pltpu.VMEM((PICK, BS + EXTRA, BS), jnp.int16),
            dma((6,)),
            dma((6,)),
            dma((24,)),
            dma((24,)),
            dma((8,)),
            dma((4,)),
            dma((4,)),
            dma((4,)),
            dma((12,)),
            dma((12,)),
        ],
        compiler_params=pltpu.CompilerParams(
            collective_id=0, has_side_effects=True, vmem_limit_bytes=32 * 1024 * 1024
        ),
    )(*[pltpu.with_memory_space_constraint(a, pltpu.HBM) for a in arrays])


def solution(mesh):
    every = ("row", "col", "layer")
    in_specs = (P(("row", "col"), None, None), P(every), P(every), P(every, None), P(every, None), P(every))
    out_specs = P(every, None, None)
    return jax.shard_map(shards, mesh=mesh, in_specs=in_specs, out_specs=out_specs, check_vma=False)
```

```python
import functools

import jax
import jax.numpy as jnp
from jax import lax
from jax.experimental import pallas as pl
from jax.experimental.pallas import tpu as pltpu
from jax.sharding import PartitionSpec as P

MESH = pl.DeviceIdType.MESH
BS = 128
PICK = 4
SLOTS = 16
TERMS = 24
LEVELS = 32760.0
EXTRA = 16
N_ROW = 16
N_COL = 8
N_LAYER = 4
N_LEFT = N_COL * PICK
N_RIGHT = N_ROW * PICK


def kernel(
    blocks_in,
    left_pick_in,
    right_pick_in,
    term_left_in,
    term_right_in,
    term_count_in,
    out,
    blocks,
    left_pick,
    right_pick,
    term_left,
    term_right,
    term_count,
    in_sem,
    left,
    right,
    part,
    packed,
    from_down,
    from_up,
    last_down,
    last_up,
    z_send,
    z_recv,
    x_send,
    x_recv,
    l_send,
    l_recv,
    c_send,
    c_recv,
    y_send,
    y_recv,
):
    row = lax.axis_index("row")
    col = lax.axis_index("col")
    layer = lax.axis_index("layer")
    z_hi, x = row // 4, row % 4
    z_lo, core = col // 2, col % 2

    def at_z(step):
        return (((z_hi + step) % 4) * 4 + x, col, layer)

    def at_x(step):
        return (z_hi * 4 + (x + step) % 4, col, layer)

    def at_line(step):
        return (row, ((z_lo + step) % 4) * 2 + core, layer)

    def at_y(step):
        return (row, col, (layer + step) % 4)

    sibling = (row, z_lo * 2 + 1 - core, layer)

    pairs = [
        (left_pick_in, left_pick),
        (right_pick_in, right_pick),
        (blocks_in, blocks),
        (term_left_in, term_left),
        (term_right_in, term_right),
        (term_count_in, term_count),
    ]
    loads = [pltpu.make_async_copy(src, dst, in_sem.at[i]) for i, (src, dst) in enumerate(pairs)]
    for load in loads:
        load.start()
    barrier = pltpu.get_barrier_semaphore()
    partners = [at_z(1), at_z(3), at_x(1), at_x(2), at_x(3), sibling, at_y(1), at_y(3)]
    for partner in partners:
        pl.semaphore_signal(barrier, inc=1, device_id=partner, device_id_type=MESH)

    @pl.when(z_lo < 3)
    def _():
        pl.semaphore_signal(barrier, inc=1, device_id=at_line(1), device_id_type=MESH)

    @pl.when(z_lo > 0)
    def _():
        pl.semaphore_signal(barrier, inc=1, device_id=at_line(3), device_id_type=MESH)

    for load in loads[:3]:
        load.wait()
    for j in range(PICK):
        right[row * PICK + j] = blocks[right_pick[j]]
    for j in range(PICK):
        left[col * PICK + j] = blocks[left_pick[j]]
    left[N_LEFT] = jnp.zeros((BS, BS), jnp.bfloat16)
    inner = jnp.where((z_lo > 0) & (z_lo < 3), 1, 0)
    pl.semaphore_wait(barrier, len(partners) + 1 + inner)

    def copy(ref, first, count, send, recv, target):
        return pltpu.make_async_remote_copy(
            src_ref=ref.at[pl.ds(first, count)],
            dst_ref=ref.at[pl.ds(first, count)],
            send_sem=send,
            recv_sem=recv,
            device_id=target,
            device_id_type=MESH,
        )

    def first_of(h, xx, half):
        return (((h + 4) % 4) * 4 + (xx + 4) % 4) * PICK + 2 * half

    def z_copy(h, half, step, k):
        return copy(right, first_of(h, x, half), 2, z_send.at[k], z_recv.at[k], at_z(step))

    def x_copy(dz, half, step, xx):
        k = (dz * 2 + half) * 3 + step - 1
        return copy(right, first_of(z_hi + dz, xx, half), 2, x_send.at[k], x_recv.at[k], at_x(step))

    def x_start(dz, half):
        for step in (1, 3, 2):
            x_copy(dz, half, step, x).start()

    def x_end(dz, half):
        for step in (1, 3, 2):
            x_copy(dz, half, step, x - step).wait_recv()

    def l_copy(place, step):
        k = 2 * place + (0 if step == 1 else 1)
        return copy(left, (place * 2 + core) * PICK, PICK, l_send.at[k], l_recv.at[place], at_line(step))

    def l_start():
        @pl.when(z_lo < 3)
        def _():
            l_copy(z_lo, 1).start()

        @pl.when(z_lo > 0)
        def _():
            l_copy(z_lo, 3).start()

    def c_copy(place, side):
        return copy(left, (place * 2 + side) * PICK, PICK, c_send.at[place], c_recv.at[place], sibling)

    def l_pass(distance):
        @pl.when(z_lo >= distance)
        def _():
            place = z_lo - distance
            l_copy(place, 1).wait_recv()

            @pl.when(z_lo < 3)
            def _():
                l_copy(place, 1).start()

            c_copy(place, core).start()

        @pl.when(z_lo + distance <= 3)
        def _():
            place = z_lo + distance
            l_copy(place, 3).wait_recv()

            @pl.when(z_lo > 0)
            def _():
                l_copy(place, 3).start()

            c_copy(place, core).start()

    z_copy(z_hi, 0, 1, 0).start()
    z_copy(z_hi, 1, 3, 1).start()
    x_start(0, 0)
    x_start(0, 1)
    c_copy(z_lo, core).start()
    z_copy(z_hi, 0, 1, 0).wait_send()
    z_copy(z_hi, 1, 1, 2).start()
    z_copy(z_hi, 1, 3, 1).wait_send()
    z_copy(z_hi, 0, 3, 3).start()
    l_start()
    z_copy(z_hi + 3, 0, 1, 0).wait_recv()
    z_copy(z_hi + 3, 0, 1, 4).start()
    x_start(3, 0)
    z_copy(z_hi + 1, 1, 3, 1).wait_recv()
    z_copy(z_hi + 1, 1, 3, 5).start()
    x_start(1, 1)
    z_copy(z_hi + 3, 1, 1, 2).wait_recv()
    x_start(3, 1)
    z_copy(z_hi + 1, 0, 3, 3).wait_recv()
    x_start(1, 0)
    l_pass(1)
    z_copy(z_hi + 2, 0, 1, 4).wait_recv()
    x_start(2, 0)
    l_pass(2)
    z_copy(z_hi + 2, 1, 3, 5).wait_recv()
    x_start(2, 1)
    l_pass(3)
    for dz in (0, 3, 1, 2):
        for half in range(2):
            x_end(dz, half)
    for place in range(4):
        c_copy(place, 1 - core).wait_recv()
    for load in loads[3:]:
        load.wait()

    def product(s):
        count = term_count[s]
        total = None
        for t in range(0, TERMS, 2):
            ids = [jnp.where(t + i < count, term_left[s, t + i], N_LEFT) for i in range(2)]
            lhs = jnp.concatenate([left[i] for i in ids], axis=1)
            rhs = jnp.concatenate([right[term_right[s, t + i]] for i in range(2)], axis=0)
            now = jnp.dot(lhs, rhs, preferred_element_type=jnp.float32)
            total = now if total is None else total + now
        return total

    def code(value):
        top = jnp.max(jnp.abs(value), axis=0, keepdims=True)
        power = jnp.clip(jnp.ceil(jnp.log2(top)), -120.0, 120.0)
        digits = jnp.floor(value * (jnp.exp2(-power) * LEVELS) + 0.5)
        return digits.astype(jnp.int32).astype(jnp.int16), jnp.broadcast_to(power, (EXTRA, BS)).astype(jnp.int32).astype(jnp.int16)

    def put(j, value):
        digits, power = code(value)
        packed[j, pl.ds(0, BS)] = digits
        packed[j, pl.ds(BS, EXTRA)] = power

    def get(ref, j):
        power = ref[j, pl.ds(BS, EXTRA)].astype(jnp.int32).astype(jnp.float32)[0:1]
        return ref[j, pl.ds(0, BS)].astype(jnp.int32).astype(jnp.float32) * (jnp.exp2(power) * (1.0 / LEVELS))

    def y_copy(i, dst, j, k, step):
        return pltpu.make_async_remote_copy(
            src_ref=packed.at[i],
            dst_ref=dst.at[j],
            send_sem=y_send.at[k],
            recv_sem=y_recv.at[k],
            device_id=at_y(step),
            device_id_type=MESH,
        )

    far = ((layer + 2) % 4) * PICK
    up = ((layer + 1) % 4) * PICK
    down = ((layer + 3) % 4) * PICK
    own = layer * PICK

    def far_up(j):
        return y_copy(j, from_down, j, j, 1)

    def far_down(j):
        return y_copy(2 + j, from_up, j, 2 + j, 3)

    def near_up(j):
        return y_copy(4 + j, last_down, j, 4 + j, 1)

    def near_down(j):
        return y_copy(8 + j, last_up, j, 8 + j, 3)

    @pl.loop(0, 2)
    def _(j):
        one, two = product(far + j), product(far + 2 + j)
        put(j, one)
        put(2 + j, two)
        far_up(j).start()
        far_down(j).start()

    for j in range(2):
        put(6 + j, product(up + 2 + j))
        put(8 + j, product(down + j))
    for j in range(2):
        near_up(2 + j).start()
        near_down(j).start()
    sums = [(product(up + j), product(down + 2 + j)) for j in range(2)]
    for j in range(2):
        far_up(j).wait_recv()
        put(4 + j, sums[j][0] + get(from_down, j))
        near_up(j).start()
        far_down(j).wait_recv()
        put(10 + j, sums[j][1] + get(from_up, j))
        near_down(2 + j).start()
    for j in range(PICK):
        part[j] = product(own + j)
    for j in (2, 3, 0, 1):
        near_up(j).wait_recv()
        near_down((j + 2) % 4).wait_recv()
    for j in range(PICK):
        out[j] = part[j] + get(last_down, j) + get(last_up, j)

    z_copy(z_hi, 1, 1, 2).wait_send()
    z_copy(z_hi, 0, 3, 3).wait_send()
    z_copy(z_hi + 3, 0, 1, 4).wait_send()
    z_copy(z_hi + 1, 1, 3, 5).wait_send()
    for dz in range(4):
        for half in range(2):
            for step in (1, 2, 3):
                x_copy(dz, half, step, x).wait_send()
    for place in range(4):

        @pl.when((place <= z_lo) & (z_lo < 3))
        def _():
            l_copy(place, 1).wait_send()

        @pl.when((place >= z_lo) & (z_lo > 0))
        def _():
            l_copy(place, 3).wait_send()

        c_copy(place, core).wait_send()
    for j in range(2):
        far_up(j).wait_send()
        far_down(j).wait_send()
    for j in range(PICK):
        near_up(j).wait_send()
        near_down(j).wait_send()


def shards(*arrays):
    vmem = pl.BlockSpec(memory_space=pltpu.VMEM)
    dma = pltpu.SemaphoreType.DMA
    return pl.pallas_call(
        kernel,
        out_shape=jax.ShapeDtypeStruct((PICK, BS, BS), jnp.float32),
        in_specs=[pl.BlockSpec(memory_space=pl.ANY)] * 6,
        out_specs=vmem,
        scratch_shapes=[
            pltpu.VMEM((SLOTS, BS, BS), jnp.bfloat16),
            pltpu.SMEM((PICK,), jnp.int32),
            pltpu.SMEM((PICK,), jnp.int32),
            pltpu.SMEM((SLOTS, TERMS), jnp.int32),
            pltpu.SMEM((SLOTS, TERMS), jnp.int32),
            pltpu.SMEM((SLOTS,), jnp.int32),
            dma((6,)),
            pltpu.VMEM((N_LEFT + 1, BS, BS), jnp.bfloat16),
            pltpu.VMEM((N_RIGHT, BS, BS), jnp.bfloat16),
            pltpu.VMEM((PICK, BS, BS), jnp.float32),
            pltpu.VMEM((3 * PICK, BS + EXTRA, BS), jnp.int16),
            pltpu.VMEM((2, BS + EXTRA, BS), jnp.int16),
            pltpu.VMEM((2, BS + EXTRA, BS), jnp.int16),
            pltpu.VMEM((PICK, BS + EXTRA, BS), jnp.int16),
            pltpu.VMEM((PICK, BS + EXTRA, BS), jnp.int16),
            dma((6,)),
            dma((6,)),
            dma((24,)),
            dma((24,)),
            dma((8,)),
            dma((4,)),
            dma((4,)),
            dma((4,)),
            dma((12,)),
            dma((12,)),
        ],
        compiler_params=pltpu.CompilerParams(
            collective_id=0, has_side_effects=True, vmem_limit_bytes=32 * 1024 * 1024
        ),
    )(*[pltpu.with_memory_space_constraint(a, pltpu.HBM) for a in arrays])


def solution(mesh):
    every = ("row", "col", "layer")
    in_specs = (P(("row", "col"), None, None), P(every), P(every), P(every, None), P(every, None), P(every))
    out_specs = P(every, None, None)
    return jax.shard_map(shards, mesh=mesh, in_specs=in_specs, out_specs=out_specs, check_vma=False)
```
